32 devices in a mesh: gx: 4 (over z), gy: 8 (over y, x, core).
Axes of the slice: x: 2, y: 2, z: 4, core: 2. Of those that a mesh axis runs over, the one named last changes fastest.
Arguments:
- velocity: float32 [3, 16, 1024, 1024], P(None, 'gx', 'gy'), may hold values from -6 to 6
- section: float32 [3, 16, 1024, 1024], P(None, 'gx', 'gy'), may hold values from -8 to 8
- diffusion: float32 [1024], replicated, may hold values from 1000 to 10000
- rhs_near: float32 [1024], P('gy'), may hold values from 0.6 to 1.2
- rhs_far: float32 [1024], P('gy'), may hold values from -0.2 to -0.05
- part_vel: float32 [3, 65536], P(None, ('gx', 'gy')), may hold values from -6 to 6
- part_rate: float32 [65536], P(('gx', 'gy')), may hold values from 0.5 to 5
- counts: int32 [32, 32], P(('gx', 'gy')), may hold values from 0 to 64, as said below
- cell_slot: int32 [32, 2048], P(('gx', 'gy')), may hold values from 0 to 524287
Outputs:
- velocity_new: float32 [3, 16, 1024, 1024], P(None, 'gx', 'gy')
- section_new: float32 [3, 16, 1024, 1024], P(None, 'gx', 'gy')
- part_new: float32 [3, 65536], P(None, ('gx', 'gy'))
The draws below stay inside these ranges and needn't reach their ends.
Inputs may be any that keep to these rules, and one draw needn't show every extreme that they name: counts[d, s] is the number of live slots, from the front, of the block that device s sends to device d; in every draw one receiving device gets 64 live slots from every sender.
All inputs are finite; a program needn't handle non-finite values.
Results may differ from the reference program's by a relative error of at most 0.0003.
The reference program's roundings to bfloat16 on the way (of `velocity_bf` and `push`) count: a program that leaves them out, or rounds other values in their place, can miss the bound.
Values sent between devices are 32-bit elements; how exact they have to be, the bound alone decides.
A program may use at most 192 MiB of HBM per device.

```python
import math
import jax
import jax.numpy as jnp

CX = 4
NY = 1024
CZ = 1024
SLOTS = 64
NX = 16
CY = 128
N_GX = 4
N_GY = 8
DEVICES = 32


def draw_counts(key, part):
    key_level, key_dense, key_raw, key_star = jax.random.split(key, 4)
    level_cap = jax.random.randint(key_level, (DEVICES,), 0, SLOTS + 1)
    dense_flag = jax.random.randint(key_dense, (DEVICES,), 0, 2)
    raw_count = jax.random.randint(key_raw, (DEVICES, DEVICES), 0, SLOTS + 1)
    capped = jnp.minimum(raw_count, (level_cap * dense_flag)[:, None])
    star_row = jax.random.randint(key_star, (), 0, DEVICES)
    row_ids = jnp.arange(DEVICES)[:, None]
    return jnp.where(row_ids == star_row, SLOTS, capped).astype(jnp.int32)


def draw_diffusion(key, part):
    key_amp, key_phase, key_rough = jax.random.split(jax.random.fold_in(key, 11), 3)
    rows = (jnp.arange(NY, dtype=jnp.float32) + 0.5) / NY
    amps = jax.random.uniform(key_amp, (3,), jnp.float32, -1.0, 1.0)
    phases = jax.random.uniform(key_phase, (3,), jnp.float32, 0.0, 6.2831853)
    orders = jnp.arange(1, 4, dtype=jnp.float32)
    waves = jnp.sin(jnp.pi * orders[:, None] * rows[None, :] + phases[:, None])
    smooth = (amps[0] * waves[0] + amps[1] * waves[1] + amps[2] * waves[2]) / 3.0
    rough = jax.random.uniform(key_rough, (NY,), jnp.float32, -1.0, 1.0)
    exponent = 3.5 + 0.35 * smooth + 0.15 * rough
    return jnp.exp(exponent * 2.302585093).astype(jnp.float32)


def draw_section(key, part):
    key_rough, key_level = jax.random.split(jax.random.fold_in(key, 23))
    rows = (jnp.arange(NY, dtype=jnp.float32) + 0.5) / NY
    profile = jnp.sin(jnp.pi * rows)[None, None, :, None]
    rough = jnp.clip(jax.random.normal(key_rough, (3, NX, NY, CZ), jnp.float32), -5.0, 5.0)
    level = jnp.clip(jax.random.normal(key_level, (3, NX, 1, CZ), jnp.float32), -2.5, 2.5)
    return (rough + level * profile).astype(jnp.float32)


def touch_ends(entries, rng, least, largest):
    index_at = [jax.random.randint(jax.random.fold_in(rng, axis), (), 0, length) for axis, length in enumerate(entries.shape)]
    longest = entries.shape.index(max(entries.shape))
    beside = index_at[:longest] + [(index_at[longest] + 1) % entries.shape[longest]] + index_at[longest + 1:]
    return entries.at[tuple(index_at)].set(least).at[tuple(beside)].set(largest)


def block_levels(own_key, dims, shards, least, high):
    loudness, own = 1.0, jax.random.fold_in(own_key, 6)
    for position, parts in shards:
        draws = jnp.exp(jax.random.uniform(jax.random.fold_in(own, position), (parts,), jnp.float32, least / len(shards), high / len(shards)))
        loudness = loudness * jnp.repeat(draws, dims[position] // parts).reshape([-1 if axis == position else 1 for axis in range(len(dims))])
    return loudness


def gaussian(key, extent, width, most, cuts=(), held_as=jnp.bfloat16):
    array = jax.random.normal(key, extent, jnp.float32) * width
    if len(cuts) > 0:
        array = block_levels(key, extent, cuts, -0.22, 0.18) * array
    return jnp.clip(array, min=-most, max=most).astype(held_as)


def setup_inputs(seed: int = 0) -> dict:
    key_list = jax.random.split(jax.random.key(seed), 10)
    return {
        "velocity": gaussian(key_list[0], (3, NX, NY, CZ), 1.0, 6.0, ((1, 4), (2, 8)), jnp.float32),
        "section": draw_section(jax.random.fold_in(key_list[9], 71), 0),
        "diffusion": draw_diffusion(jax.random.fold_in(key_list[9], 71), 0),
        "rhs_near": jnp.clip(0.6 + 0.6 * jax.random.uniform(key_list[3], (NY,), jnp.float32) ** block_levels(key_list[3], (NY,), ((0, 8),), -0.2, 0.2), 0.6, 1.2),
        "rhs_far": jnp.clip(-0.2 + 0.15 * jax.random.uniform(key_list[4], (NY,), jnp.float32) ** block_levels(key_list[4], (NY,), ((0, 8),), -0.2, 0.2), -0.2, -0.05),
        "part_vel": gaussian(key_list[5], (3, DEVICES * DEVICES * SLOTS), 1.0, 6.0, ((1, 32),), jnp.float32),
        "part_rate": jnp.clip(jnp.exp(math.log(5.0) - 2.3025851 * jax.random.uniform(key_list[6], (DEVICES * DEVICES * SLOTS,), jnp.float32) ** block_levels(key_list[6], (DEVICES * DEVICES * SLOTS,), ((0, 32),), -0.2, 0.2)), 0.5, 5.0),
        "counts": draw_counts(jax.random.fold_in(key_list[9], 71), 0),
        "cell_slot": touch_ends(jax.random.randint(key_list[8], (DEVICES, DEVICES * SLOTS), 0, CX * CY * CZ), jax.random.fold_in(key_list[8], 1), 0, (CX * CY * CZ) - 1).astype(jnp.int32),
    }


def reference(velocity, section, diffusion, rhs_near, rhs_far, part_vel, part_rate, counts, cell_slot):
    devices_all = N_GX * N_GY
    velocity_bf = velocity.astype(jnp.bfloat16)
    moved_vel = part_vel.reshape(3, devices_all, devices_all, SLOTS).transpose(0, 2, 1, 3).reshape(3, -1)
    moved_rate = part_rate.reshape(devices_all, devices_all, SLOTS).transpose(1, 0, 2).reshape(-1)
    slot_ids = jnp.arange(devices_all * devices_all * SLOTS, dtype=jnp.int32)
    target = slot_ids // (devices_all * SLOTS)
    source = slot_ids // SLOTS % devices_all
    within = slot_ids % SLOTS
    live = within < counts[target, source]
    cell_ids = cell_slot.reshape(-1)
    global_x = target // N_GY * CX + cell_ids // (CY * CZ)
    global_y = target % N_GY * CY + cell_ids // CZ % CY
    global_z = cell_ids % CZ
    fluid_at = velocity_bf[:, global_x, global_y, global_z].astype(jnp.float32)
    relative = fluid_at - moved_vel
    part_new = jnp.where(live[None], moved_vel + 0.2 * moved_rate[None] * relative, 0.0)
    push = jnp.where(live[None], -moved_rate[None] * relative, 0.0).astype(jnp.bfloat16)
    deposit = jnp.zeros_like(velocity).at[:, global_x, global_y, global_z].add(push.astype(velocity.dtype))

    def central(field, axis_id):
        return (8.0 * (jnp.roll(field, -1, axis_id) - jnp.roll(field, 1, axis_id)) - (jnp.roll(field, -2, axis_id) - jnp.roll(field, 2, axis_id))) / 12.0
    ddx = central(velocity, 1)
    ddz = central(velocity, 3)
    padded = jnp.pad(velocity, ((0, 0), (0, 0), (2, 2), (0, 0)))
    ddy = rhs_near[None, None, :, None] * (padded[:, :, 3:NY + 3] - padded[:, :, 1:NY + 1]) + rhs_far[None, None, :, None] * (padded[:, :, 4:] - padded[:, :, :NY])
    rhs = -(velocity[0:1] * ddx + velocity[1:2] * ddy + velocity[2:3] * ddz) + deposit
    section_new = -5.0 / 9.0 * section + 0.2 * rhs
    main_diag = 1.0 + 2.5 * diffusion
    near_coef = -4.0 / 3.0 * diffusion
    far_coef = diffusion / 12.0
    system = jnp.diag(main_diag) + jnp.diag(near_coef[1:], -1) + jnp.diag(near_coef[:-1], 1) + jnp.diag(far_coef[2:], -2) + jnp.diag(far_coef[:-2], 2)
    lines = jnp.moveaxis(15.0 / 16.0 * section_new, 2, 0).reshape(NY, -1)
    solved = jnp.linalg.solve(system, lines)
    increment = jnp.moveaxis(solved.reshape(NY, 3, NX, CZ), 0, 2)
    velocity_new = velocity + increment
    return (velocity_new, section_new, part_new)
```

```python
import jax
import jax.numpy as jnp
from jax import lax
from jax.experimental import pallas as pl
from jax.experimental.pallas import tpu as pltpu
from jax.sharding import PartitionSpec as P

HIGH = lax.Precision.HIGHEST
TIME_STEP = 0.2
SECTION_KEEP = -5.0 / 9.0
SECTION_GAIN = 15.0 / 16.0
MAIN_WEIGHT = 2.5
NEAR_WEIGHT = -4.0 / 3.0
FAR_WEIGHT = 1.0 / 12.0


def extended(block, sides, width, periodic):
    for axis, dim in sides:
        count = lax.axis_size(axis)
        forward = [(i, i + 1) for i in range(count - 1)]
        if periodic:
            forward.append((count - 1, 0))
        backward = [(target, source) for source, target in forward]
        low = lax.ppermute(
            lax.slice_in_dim(block, block.shape[dim] - width, None, axis=dim), axis, forward
        )
        high = lax.ppermute(lax.slice_in_dim(block, 0, width, axis=dim), axis, backward)
        block = jnp.concatenate([low, block, high], axis=dim)
    return block


def band_inverse_kernel(rate_ref, inverse_ref, near_ref, far_ref):
    rows, slabs, columns = rate_ref.shape
    lanes = lax.broadcasted_iota(jnp.int32, (slabs, columns), 1)
    zero = 0.0 * rate_ref[0]

    def down(row, carry):
        near_a, far_a, value_a, near_b, far_b, value_b = carry
        rate = rate_ref[row]
        near = NEAR_WEIGHT * rate
        far = FAR_WEIGHT * rate
        low = near - far * near_b
        pivot = (1.0 + MAIN_WEIGHT * rate) - far * far_b - low * near_a
        scale = 1.0 / pivot
        unit = jnp.where(lanes == row, 1.0, 0.0)
        near_here = (near - low * far_a) * scale
        far_here = far * scale
        value = (unit - far * value_b - low * value_a) * scale
        near_ref[row] = near_here
        far_ref[row] = far_here
        inverse_ref[row] = value
        return (near_here, far_here, value, near_a, far_a, value_a)

    lax.fori_loop(0, rows, down, (zero,) * 6)

    def up(step, carry):
        row = rows - 1 - step
        value_a, value_b = carry
        value = inverse_ref[row] - near_ref[row] * value_a - far_ref[row] * value_b
        inverse_ref[row] = value
        return (value, value_a)

    lax.fori_loop(0, rows, up, (zero, zero))


def band_inverse(rate):
    slabs, rows = rate.shape
    spread = jnp.broadcast_to(rate.T[:, :, None], (rows, slabs, rows))
    return pl.pallas_call(
        band_inverse_kernel,
        out_shape=jax.ShapeDtypeStruct((rows, slabs, rows), jnp.float32),
        in_specs=[pl.BlockSpec(memory_space=pltpu.VMEM)],
        out_specs=pl.BlockSpec(memory_space=pltpu.VMEM),
        scratch_shapes=[pltpu.VMEM((rows, slabs, rows), jnp.float32)] * 2,
        compiler_params=pltpu.CompilerParams(vmem_limit_bytes=16 * 2**20),
    )(spread)


def small_inverse_kernel(matrix_ref, inverse_ref):
    extent = matrix_ref.shape[0]
    lanes = lax.broadcasted_iota(jnp.int32, (extent, extent), 1)
    heights = lax.broadcasted_iota(jnp.int32, (extent, extent), 0)
    lane_row = lax.broadcasted_iota(jnp.int32, (1, extent), 1)
    inverse_ref[...] = matrix_ref[...]

    def eliminate(index, carry):
        matrix = inverse_ref[...]
        head = inverse_ref[pl.ds(index, 1), :]
        pivot = jnp.sum(jnp.where(lane_row == index, head, 0.0), axis=1, keepdims=True)
        head = jnp.where(lane_row == index, 1.0, head) / pivot
        column = jnp.sum(jnp.where(lanes == index, matrix, 0.0), axis=1, keepdims=True)
        rest = jnp.where(lanes == index, 0.0, matrix) - column * head
        inverse_ref[...] = jnp.where(heights == index, jnp.broadcast_to(head, rest.shape), rest)
        return carry

    lax.fori_loop(0, extent, eliminate, 0)


def small_inverse(matrix):
    return pl.pallas_call(
        small_inverse_kernel,
        out_shape=jax.ShapeDtypeStruct(matrix.shape, jnp.float32),
        in_specs=[pl.BlockSpec(memory_space=pltpu.VMEM)],
        out_specs=pl.BlockSpec(memory_space=pltpu.VMEM),
        compiler_params=pltpu.CompilerParams(vmem_limit_bytes=16 * 2**20),
    )(matrix)


def wall_factors(diffusion, slabs, slab_rows, slab_index):
    rate = diffusion.reshape(slabs, slab_rows)
    near = NEAR_WEIGHT * rate
    far = FAR_WEIGHT * rate
    inverse = band_inverse(rate)
    last = slab_rows - 1

    def low_fix(block, scale_near, scale_far):
        first, second = block[..., 0], block[..., 1]
        return jnp.stack(
            [first * scale_far[:, 0], first * scale_near[:, 0] + second * scale_far[:, 1]], axis=-1
        )

    def high_fix(block, scale_near, scale_far):
        final, ahead = block[..., -1], block[..., -2]
        return jnp.stack(
            [
                ahead * scale_far[:, last - 1] + final * scale_near[:, last],
                final * scale_far[:, last],
            ],
            axis=-1,
        )

    tip = jnp.concatenate([inverse[0:2], inverse[last - 1 :]], axis=0)
    tip_low = jnp.swapaxes(low_fix(tip, near, far), 0, 1)
    tip_high = jnp.swapaxes(high_fix(tip, near, far), 0, 1)
    zeros_half = jnp.zeros((slabs, 4, 2), jnp.float32)
    link_down = jnp.concatenate([zeros_half, tip_low], axis=2)
    link_up = jnp.concatenate([tip_high, zeros_half], axis=2)
    extent = 4 * slabs
    below = jnp.eye(slabs, k=-1, dtype=jnp.float32)[:, None, :, None]
    above = jnp.eye(slabs, k=1, dtype=jnp.float32)[:, None, :, None]
    system = (
        below * link_down[:, :, None, :] + above * link_up[:, :, None, :]
    ).reshape(extent, extent) + jnp.eye(extent, dtype=jnp.float32)
    settled = jnp.pad(small_inverse(system), ((4, 4), (0, 0)))
    low_rows = lax.dynamic_slice_in_dim(settled, 4 * slab_index + 2, 2, 0)
    high_rows = lax.dynamic_slice_in_dim(settled, 4 * slab_index + 8, 2, 0)
    own = lax.dynamic_index_in_dim(inverse, slab_index, 1, keepdims=False)
    own_near = lax.dynamic_slice_in_dim(near, slab_index, 1, 0)
    own_far = lax.dynamic_slice_in_dim(far, slab_index, 1, 0)
    lower_fix = low_fix(own, own_near, own_far)
    upper_fix = high_fix(own, own_near, own_far)
    fix = -(
        lower_fix[:, 0:1] * low_rows[0:1]
        + lower_fix[:, 1:2] * low_rows[1:2]
        + upper_fix[:, 0:1] * high_rows[0:1]
        + upper_fix[:, 1:2] * high_rows[1:2]
    )
    return own, fix


def central(field, axis_id):
    return (
        8.0 * (jnp.roll(field, -1, axis_id) - jnp.roll(field, 1, axis_id))
        - (jnp.roll(field, -2, axis_id) - jnp.roll(field, 2, axis_id))
    ) / 12.0


def local(velocity, section, diffusion, rhs_near, rhs_far, part_vel, part_rate, counts, cell_slot):
    components, width_x, slab_rows, width_z = velocity.shape
    slabs = lax.axis_size("gy")
    slab_index = lax.axis_index("gy")
    devices_all = counts.shape[1]
    total_slots = part_vel.shape[1]
    slot_count = total_slots // devices_all
    planes = width_x * slab_rows
    moved_vel, moved_rate = (
        lax.all_to_all(part_vel, ("gx", "gy"), split_axis=1, concat_axis=1, tiled=True),
        lax.all_to_all(
            part_rate.reshape(1, total_slots), ("gx", "gy"), split_axis=1, concat_axis=1, tiled=True
        ),
    )
    live = jnp.arange(total_slots) % slot_count < jnp.repeat(
        counts[0], slot_count, total_repeat_length=total_slots
    )
    cell_ids = cell_slot[0]
    plane_ids = cell_ids // width_z
    span_ids = cell_ids % width_z
    span_table = (jnp.arange(width_z)[:, None] == span_ids[None, :]).astype(jnp.bfloat16)
    plane_table = jnp.arange(planes)[:, None] == plane_ids[None, :]
    velocity_bf = velocity.astype(jnp.bfloat16).reshape(components * planes, width_z)
    at_cells = jnp.einsum("hz,zp->hp", velocity_bf, span_table, preferred_element_type=jnp.float32)
    fluid_at = jnp.sum(
        at_cells.reshape(components, planes, total_slots) * plane_table.astype(jnp.float32)[None],
        axis=1,
    )
    relative = fluid_at - moved_vel
    part_new = jnp.where(live[None], moved_vel + TIME_STEP * moved_rate * relative, 0.0)
    push = jnp.where(live[None], -moved_rate * relative, 0.0).astype(jnp.bfloat16)
    spread = (push[:, None, :] * plane_table.astype(jnp.bfloat16)[None]).reshape(
        components * planes, total_slots
    )
    deposit = jnp.einsum("hp,zp->hz", spread, span_table, preferred_element_type=jnp.float32)
    deposit = deposit.reshape(components, width_x, slab_rows, width_z)
    axial_pad = extended(velocity, (("gx", 1),), 2, True)
    ddx = (
        8.0 * (axial_pad[:, 3 : width_x + 3] - axial_pad[:, 1 : width_x + 1])
        - (axial_pad[:, 4:] - axial_pad[:, :width_x])
    ) / 12.0
    ddz = central(velocity, 3)
    wall_pad = extended(velocity, (("gy", 2),), 2, False)
    ddy = rhs_near[None, None, :, None] * (
        wall_pad[:, :, 3 : slab_rows + 3] - wall_pad[:, :, 1 : slab_rows + 1]
    ) + rhs_far[None, None, :, None] * (wall_pad[:, :, 4:] - wall_pad[:, :, :slab_rows])
    rhs = -(velocity[0:1] * ddx + velocity[1:2] * ddy + velocity[2:3] * ddz) + deposit
    section_new = SECTION_KEEP * section + TIME_STEP * rhs
    source = SECTION_GAIN * section_new
    inverse_band, fix = wall_factors(diffusion, slabs, slab_rows, slab_index)
    tip_inverse = jnp.concatenate([inverse_band[0:2], inverse_band[slab_rows - 2 :]], axis=0)
    tips = jnp.einsum("mk,cxkz->cxmz", tip_inverse, source, precision=HIGH)
    all_tips = lax.all_gather(tips, "gy", axis=2, tiled=True)
    increment = jnp.einsum("jk,cxkz->cxjz", inverse_band, source, precision=HIGH) + jnp.einsum(
        "jm,cxmz->cxjz", fix, all_tips, precision=HIGH
    )
    velocity_new = velocity + increment
    return (velocity_new, section_new, part_new)


def solution(mesh):
    return jax.shard_map(
        local,
        mesh=mesh,
        in_specs=(
            P(None, "gx", "gy", None),
            P(None, "gx", "gy", None),
            P(),
            P("gy"),
            P("gy"),
            P(None, ("gx", "gy")),
            P(("gx", "gy")),
            P(("gx", "gy"), None),
            P(("gx", "gy"), None),
        ),
        out_specs=(P(None, "gx", "gy", None), P(None, "gx", "gy", None), P(None, ("gx", "gy"))),
        check_vma=False,
    )
```

```python
import functools
import jax
import jax.numpy as jnp
from jax import lax
from jax.experimental import pallas as pl
from jax.experimental.pallas import tpu as pltpu
from jax.sharding import PartitionSpec as P

HIGH = lax.Precision.HIGHEST
TIME_STEP = 0.2
SECTION_KEEP = -5.0 / 9.0
SECTION_GAIN = 15.0 / 16.0
MAIN_WEIGHT = 2.5
NEAR_WEIGHT = -4.0 / 3.0
FAR_WEIGHT = 1.0 / 12.0


def extended(block, sides, width, periodic, after=None):
    for axis, dim in sides:
        count = lax.axis_size(axis)
        forward = [(i, i + 1) for i in range(count - 1)]
        if periodic:
            forward.append((count - 1, 0))
        backward = [(target, source) for source, target in forward]
        top = lax.slice_in_dim(block, block.shape[dim] - width, None, axis=dim)
        bottom = lax.slice_in_dim(block, 0, width, axis=dim)
        if after is not None:
            top, bottom, _ = lax.optimization_barrier((top, bottom, after))
        low = lax.ppermute(top, axis, forward)
        high = lax.ppermute(bottom, axis, backward)
        block = jnp.concatenate([low, block, high], axis=dim)
    return block


def band_inverse_kernel(rate_ref, inverse_ref, near_ref, far_ref):
    rows, slabs, columns = rate_ref.shape
    lanes = lax.broadcasted_iota(jnp.int32, (slabs, columns), 1)
    zero = 0.0 * rate_ref[0]

    def down(row, carry):
        near_a, far_a, value_a, near_b, far_b, value_b = carry
        rate = rate_ref[row]
        near = NEAR_WEIGHT * rate
        far = FAR_WEIGHT * rate
        low = near - far * near_b
        pivot = (1.0 + MAIN_WEIGHT * rate) - far * far_b - low * near_a
        scale = 1.0 / pivot
        unit = jnp.where(lanes == row, 1.0, 0.0)
        near_here = (near - low * far_a) * scale
        far_here = far * scale
        value = (unit - far * value_b - low * value_a) * scale
        near_ref[row] = near_here
        far_ref[row] = far_here
        inverse_ref[row] = value
        return (near_here, far_here, value, near_a, far_a, value_a)

    lax.fori_loop(0, rows, down, (zero,) * 6)

    def up(step, carry):
        row = rows - 1 - step
        value_a, value_b = carry
        value = inverse_ref[row] - near_ref[row] * value_a - far_ref[row] * value_b
        inverse_ref[row] = value
        return (value, value_a)

    lax.fori_loop(0, rows, up, (zero, zero))


def band_inverse(rate):
    slabs, rows = rate.shape
    spread = jnp.broadcast_to(rate.T[:, :, None], (rows, slabs, rows))
    return pl.pallas_call(
        band_inverse_kernel,
        out_shape=jax.ShapeDtypeStruct((rows, slabs, rows), jnp.float32),
        in_specs=[pl.BlockSpec(memory_space=pltpu.VMEM)],
        out_specs=pl.BlockSpec(memory_space=pltpu.VMEM),
        scratch_shapes=[pltpu.VMEM((rows, slabs, rows), jnp.float32)] * 2,
        compiler_params=pltpu.CompilerParams(vmem_limit_bytes=16 * 2**20),
    )(spread)


def small_inverse_kernel(matrix_ref, inverse_ref):
    extent = matrix_ref.shape[0]
    lanes = lax.broadcasted_iota(jnp.int32, (extent, extent), 1)
    heights = lax.broadcasted_iota(jnp.int32, (extent, extent), 0)
    lane_row = lax.broadcasted_iota(jnp.int32, (1, extent), 1)
    inverse_ref[...] = matrix_ref[...]

    def eliminate(index, carry):
        matrix = inverse_ref[...]
        head = inverse_ref[pl.ds(index, 1), :]
        pivot = jnp.sum(jnp.where(lane_row == index, head, 0.0), axis=1, keepdims=True)
        head = jnp.where(lane_row == index, 1.0, head) / pivot
        column = jnp.sum(jnp.where(lanes == index, matrix, 0.0), axis=1, keepdims=True)
        rest = jnp.where(lanes == index, 0.0, matrix) - column * head
        inverse_ref[...] = jnp.where(heights == index, jnp.broadcast_to(head, rest.shape), rest)
        return carry

    lax.fori_loop(0, extent, eliminate, 0)


def small_inverse(matrix):
    return pl.pallas_call(
        small_inverse_kernel,
        out_shape=jax.ShapeDtypeStruct(matrix.shape, jnp.float32),
        in_specs=[pl.BlockSpec(memory_space=pltpu.VMEM)],
        out_specs=pl.BlockSpec(memory_space=pltpu.VMEM),
        compiler_params=pltpu.CompilerParams(vmem_limit_bytes=16 * 2**20),
    )(matrix)


def wall_factors(diffusion, slabs, slab_rows, slab_index):
    rate = diffusion.reshape(slabs, slab_rows)
    near = NEAR_WEIGHT * rate
    far = FAR_WEIGHT * rate
    inverse = band_inverse(rate)
    last = slab_rows - 1

    def low_fix(block, scale_near, scale_far):
        first, second = block[..., 0], block[..., 1]
        return jnp.stack(
            [first * scale_far[:, 0], first * scale_near[:, 0] + second * scale_far[:, 1]], axis=-1
        )

    def high_fix(block, scale_near, scale_far):
        final, ahead = block[..., -1], block[..., -2]
        return jnp.stack(
            [
                ahead * scale_far[:, last - 1] + final * scale_near[:, last],
                final * scale_far[:, last],
            ],
            axis=-1,
        )

    tip = jnp.concatenate([inverse[0:2], inverse[last - 1 :]], axis=0)
    tip_low = jnp.swapaxes(low_fix(tip, near, far), 0, 1)
    tip_high = jnp.swapaxes(high_fix(tip, near, far), 0, 1)
    zeros_half = jnp.zeros((slabs, 4, 2), jnp.float32)
    link_down = jnp.concatenate([zeros_half, tip_low], axis=2)
    link_up = jnp.concatenate([tip_high, zeros_half], axis=2)
    extent = 4 * slabs
    below = jnp.eye(slabs, k=-1, dtype=jnp.float32)[:, None, :, None]
    above = jnp.eye(slabs, k=1, dtype=jnp.float32)[:, None, :, None]
    system = (
        below * link_down[:, :, None, :] + above * link_up[:, :, None, :]
    ).reshape(extent, extent) + jnp.eye(extent, dtype=jnp.float32)
    settled = jnp.pad(small_inverse(system), ((4, 4), (0, 0)))
    low_rows = lax.dynamic_slice_in_dim(settled, 4 * slab_index + 2, 2, 0)
    high_rows = lax.dynamic_slice_in_dim(settled, 4 * slab_index + 8, 2, 0)
    own = lax.dynamic_index_in_dim(inverse, slab_index, 1, keepdims=False)
    own_near = lax.dynamic_slice_in_dim(near, slab_index, 1, 0)
    own_far = lax.dynamic_slice_in_dim(far, slab_index, 1, 0)
    lower_fix = low_fix(own, own_near, own_far)
    upper_fix = high_fix(own, own_near, own_far)
    fix = -(
        lower_fix[:, 0:1] * low_rows[0:1]
        + lower_fix[:, 1:2] * low_rows[1:2]
        + upper_fix[:, 0:1] * high_rows[0:1]
        + upper_fix[:, 1:2] * high_rows[1:2]
    )
    return own, fix


def central(field, axis_id):
    return (
        8.0 * (jnp.roll(field, -1, axis_id) - jnp.roll(field, 1, axis_id))
        - (jnp.roll(field, -2, axis_id) - jnp.roll(field, 2, axis_id))
    ) / 12.0


def couple_kernel(planes, velocity_ref, moved_ref, marks_ref, part_ref, deposit_ref):
    components = part_ref.shape[0]
    tile = part_ref.shape[1]
    width_z = velocity_ref.shape[1]

    @pl.when(pl.program_id(0) == 0)
    def _():
        deposit_ref[...] = jnp.zeros_like(deposit_ref)

    plane_ids = marks_ref[0:1, :]
    span_ids = marks_ref[1:2, :]
    live = marks_ref[2:3, :] > 0
    rate = moved_ref[components : components + 1, :]
    heights = lax.broadcasted_iota(jnp.int32, (planes, tile), 0)
    at_plane = heights == plane_ids
    spans = lax.broadcasted_iota(jnp.int32, (width_z, tile), 0)
    span_table = jnp.where(spans == span_ids, 1.0, 0.0).astype(jnp.bfloat16)
    for c in range(components):
        block = pl.ds(c * planes, planes)
        at_cells = jnp.dot(velocity_ref[block, :], span_table, preferred_element_type=jnp.float32)
        fluid_at = jnp.sum(jnp.where(at_plane, at_cells, 0.0), axis=0, keepdims=True)
        vel = moved_ref[c : c + 1, :]
        relative = fluid_at - vel
        part_ref[c : c + 1, :] = jnp.where(live, vel + TIME_STEP * rate * relative, 0.0)
        push = jnp.where(live, -rate * relative, 0.0)
        spread = jnp.where(at_plane, push, 0.0).astype(jnp.bfloat16)
        deposit_ref[block, :] += lax.dot_general(
            spread, span_table, (((1,), (1,)), ((), ())), preferred_element_type=jnp.float32
        )


def couple_particles(velocity_bf, moved, marks):
    components = moved.shape[0] - 1
    rows, width_z = velocity_bf.shape
    total = moved.shape[1]
    tile = 256
    return pl.pallas_call(
        functools.partial(couple_kernel, rows // components),
        grid=(total // tile,),
        out_shape=(
            jax.ShapeDtypeStruct((components, total), jnp.float32),
            jax.ShapeDtypeStruct((rows, width_z), jnp.float32),
        ),
        in_specs=[
            pl.BlockSpec((rows, width_z), lambda i: (0, 0)),
            pl.BlockSpec((components + 1, tile), lambda i: (0, i)),
            pl.BlockSpec((3, tile), lambda i: (0, i)),
        ],
        out_specs=(
            pl.BlockSpec((components, tile), lambda i: (0, i)),
            pl.BlockSpec((rows, width_z), lambda i: (0, 0)),
        ),
        compiler_params=pltpu.CompilerParams(vmem_limit_bytes=48 * 2**20),
        cost_estimate=pl.CostEstimate(
            flops=4 * rows * width_z * total, bytes_accessed=6 * rows * width_z, transcendentals=0
        ),
    )(velocity_bf, moved, marks)


def local(velocity, section, diffusion, rhs_near, rhs_far, part_vel, part_rate, counts, cell_slot):
    components, width_x, slab_rows, width_z = velocity.shape
    slabs = lax.axis_size("gy")
    slab_index = lax.axis_index("gy")
    devices_all = counts.shape[1]
    total_slots = part_vel.shape[1]
    slot_count = total_slots // devices_all
    planes = width_x * slab_rows
    sent = jnp.concatenate([part_vel, part_rate.reshape(1, total_slots)], axis=0)
    moved = lax.all_to_all(sent, ("gx", "gy"), split_axis=1, concat_axis=1, tiled=True)
    live = (jnp.arange(slot_count)[None, :] < counts[0][:, None]).reshape(total_slots)
    cell_ids = cell_slot[0]
    marks = jnp.stack([cell_ids // width_z, cell_ids % width_z, live.astype(jnp.int32)])
    velocity_bf = velocity.astype(jnp.bfloat16).reshape(components * planes, width_z)
    part_new, deposit = couple_particles(velocity_bf, moved, marks)
    deposit = deposit.reshape(components, width_x, slab_rows, width_z)
    axial_pad = extended(velocity, (("gx", 1),), 2, True, moved)
    layers = [axial_pad[:, i : i + 1] for i in range(width_x + 4)]
    ddx = jnp.concatenate(
        [
            (8.0 * (layers[i + 3] - layers[i + 1]) - (layers[i + 4] - layers[i])) / 12.0
            for i in range(width_x)
        ],
        axis=1,
    )
    ddz = central(velocity, 3)
    wall_pad = extended(velocity, (("gy", 2),), 2, False)
    ddy = rhs_near[None, None, :, None] * (
        wall_pad[:, :, 3 : slab_rows + 3] - wall_pad[:, :, 1 : slab_rows + 1]
    ) + rhs_far[None, None, :, None] * (wall_pad[:, :, 4:] - wall_pad[:, :, :slab_rows])
    rhs = -(velocity[0:1] * ddx + velocity[1:2] * ddy + velocity[2:3] * ddz) + deposit
    section_new = SECTION_KEEP * section + TIME_STEP * rhs
    source = SECTION_GAIN * section_new
    inverse_band, fix = wall_factors(diffusion, slabs, slab_rows, slab_index)
    tip_inverse = jnp.concatenate([inverse_band[0:2], inverse_band[slab_rows - 2 :]], axis=0)
    tips = jnp.einsum("mk,cxkz->cxmz", tip_inverse, source, precision=HIGH)
    all_tips = lax.all_gather(tips, "gy", axis=2, tiled=True)
    increment = jnp.einsum("jk,cxkz->cxjz", inverse_band, source, precision=HIGH) + jnp.einsum(
        "jm,cxmz->cxjz", fix, all_tips, precision=HIGH
    )
    velocity_new = velocity + increment
    return (velocity_new, section_new, part_new)


def solution(mesh):
    return jax.shard_map(
        local,
        mesh=mesh,
        in_specs=(
            P(None, "gx", "gy", None),
            P(None, "gx", "gy", None),
            P(),
            P("gy"),
            P("gy"),
            P(None, ("gx", "gy")),
            P(("gx", "gy")),
            P(("gx", "gy"), None),
            P(("gx", "gy"), None),
        ),
        out_specs=(P(None, "gx", "gy", None), P(None, "gx", "gy", None), P(None, ("gx", "gy"))),
        check_vma=False,
    )
```
